32 devices in a mesh: dp: 4 (over y, core), owner: 8 (over z, x).
Axes of the slice: x: 2, y: 2, z: 4, core: 2. Of those that a mesh axis runs over, the one named last changes fastest.
Arguments:
- tokens: bfloat16 [2048, 4096], P('dp'), may hold values from -6 to 6
- route: int32 [2048, 1], P('dp'), may hold values from 0 to 3; in each aligned block of 512 rows (0 to 511, 512 to 1023, ...) at most 384 rows name the same one
- gate_prob: float32 [2048], P('dp'), may hold values from 0.1 to 1
- w_gate: bfloat16 [4096, 6144], P('dp', 'owner'), may hold values from -0.09375 to 0.09375
- w_up: bfloat16 [4096, 6144], P('dp', 'owner'), may hold values from -0.09375 to 0.09375
- w_down: bfloat16 [6144, 4096], P('owner', 'dp'), may hold values from -0.15625 to 0.15625
- d_out: bfloat16 [2048, 4096], P('dp', 'owner'), may hold values from -1.5 to 1.5
Outputs:
- mixed: bfloat16 [2048, 4096], P('dp', 'owner')
- grad_tokens: bfloat16 [2048, 4096], P('dp', 'owner')
- grad_gate: float32 [2048], P('dp')
- grad_w_gate: float32 [4096, 6144], P('dp', 'owner')
- grad_w_up: float32 [4096, 6144], P('dp', 'owner')
- grad_w_down: float32 [6144, 4096], P('owner', 'dp')
The draws below stay inside these ranges and needn't reach their ends.
Inputs may be any that keep to these rules, and one draw needn't show every extreme that they name: `route`: in every aligned block of 512 rows no expert is named by more than 384 rows, and in some block one expert is named by exactly 384 rows.
All inputs are finite; a program needn't handle non-finite values.
Results may differ from the reference program's by a relative error of at most 0.017.
Values may be sent and summed in bfloat16 or wider, within the bound.
No kernel may reach another device: no remote copies, remote signals or barrier semaphores. Data moves between devices by JAX's collectives and lax.ppermute only.
A program may use at most 128 MiB of HBM per device.

```python
import math
import jax
import jax.numpy as jnp
import numpy as np
from jax import lax

D = 4096
FF = 1536
EXPERTS = 4
TOK_GRP = 512
CAP = 384
TOKENS = 2048
N_DP = 4
N_OWNER = 8


def level_of(rng, shape, cuts, smallest, top_value):
    factor_of = 1.0
    for axis_at, parts in cuts:
        draws = jax.random.uniform(jax.random.fold_in(jax.random.fold_in(rng, 6), axis_at), (parts,), jnp.float32, smallest / len(cuts), top_value / len(cuts))
        factor_of = factor_of * jnp.repeat(jnp.exp(draws), shape[axis_at] // parts).reshape((-1,) + (1,) * (len(shape) - 1 - axis_at))
    return factor_of


def shared_out(own_key, own, number, rows, amount, top, bound, lean):
    order = jax.random.permutation(own_key, amount)
    packed, ordinary = load_shares(amount, rows * top, bound, lean, True), load_shares(amount, rows * top, bound, lean, False)
    places = jnp.arange(amount)

    def named(lengths, rotation):
        used = int((lengths > 0).sum())
        fixed = max(1, used // 4)
        moved = fixed + (places - fixed + rotation * (used - fixed)) % max(1, amount - fixed)
        return jnp.zeros((amount,), jnp.int32).at[order[jnp.where(places < fixed, places, moved)]].set(jnp.asarray(lengths, jnp.int32))

    lengths = jnp.where(number % 4 == 0, named(packed, number // 4), named(ordinary, number - number // 4 - 1))
    mixed = jax.random.permutation(jax.random.fold_in(own, 3), amount)
    donor, taker = mixed[0:amount // 2 * 2:2], mixed[1:amount // 2 * 2:2]
    margin = jnp.minimum(lengths[donor] - 1, bound - lengths[taker]) // 2
    margin = jnp.where((donor == order[0]) | (taker == order[0]) | (lengths[taker] == 0), 0, jnp.maximum(margin, 0))
    moved = jax.random.randint(jax.random.fold_in(own, 4), (amount // 2,), 0, 1 << 20) % (margin + 1)
    lengths = lengths.at[donor].add(-moved).at[taker].add(moved)
    labels = jnp.searchsorted(jnp.cumsum(lengths), jnp.arange(rows * top), side="right").astype(jnp.int32)
    grid = labels.reshape(top, rows).T
    grid = grid[jax.random.permutation(jax.random.fold_in(own, 1), rows)]
    rotation = jax.random.randint(jax.random.fold_in(own, 2), (rows, 1), 0, top)
    return jnp.take_along_axis(grid, (jnp.arange(top)[None, :] + rotation) % top, axis=1)


def load_shares(count, total, limit, slope, full):
    portions = [(1 << 20) // math.isqrt(grade ** slope) + 1 for grade in range(1, count + 1)]
    largest = limit if full else min(limit, max(-(-total // count), total * portions[0] // sum(portions)))
    least = 1 if total - largest >= count - 1 else 0
    counts, surplus = [largest] + [least] * (count - 1), total - largest - least * (count - 1)
    while surplus > 0:
        movable = [i for i in range(1, count) if counts[i] < largest] or [i for i in range(1, count) if counts[i] < limit]
        pool, budget = sum([portions[i] for i in movable]), surplus
        for i in movable:
            more = min(limit - counts[i], max(1, budget * portions[i] // pool), surplus)
            counts[i] = counts[i] + more
            surplus = surplus - more
    return np.array(counts)


def normal_values(stream_key, extent, deviation, bound, split=(), held_as=jnp.bfloat16):
    drawn = jax.random.normal(stream_key, extent, jnp.float32) * deviation
    if len(split) > 0:
        drawn = level_of(stream_key, extent, split, -0.22, 0.18) * drawn
    return jnp.clip(drawn, min=-bound, max=bound).astype(held_as)


def setup_inputs(seed: int = 0) -> dict:
    streams_of = jax.random.split(jax.random.key(seed), 8)
    tokens = normal_values(streams_of[0], (TOKENS, D), 1.0, 6.0, ((0, 4),))
    route_keys = jax.random.split(jax.random.fold_in(streams_of[1], 1), TOKENS // TOK_GRP)
    route_turns = jax.random.permutation(jax.random.fold_in(streams_of[1], 3), TOKENS // TOK_GRP)
    route = jax.vmap(lambda own, number: shared_out(jax.random.fold_in(streams_of[1], 2), own, number, TOK_GRP, EXPERTS, 1, CAP, 2))(route_keys, route_turns).reshape((TOKENS, 1))
    gate_prob = jnp.clip(0.1 + 0.9 * jax.random.uniform(streams_of[2], (TOKENS,), jnp.float32) ** level_of(streams_of[2], (TOKENS,), ((0, 4),), -0.2, 0.2), 0.1, 1.0)
    w_gate = normal_values(streams_of[3], (D, EXPERTS * FF), D ** -0.5, 0.09375, ((0, 4), (1, 8)))
    w_up = normal_values(streams_of[4], (D, EXPERTS * FF), D ** -0.5, 0.09375, ((0, 4), (1, 8)))
    w_down = normal_values(streams_of[5], (EXPERTS * FF, D), FF ** -0.5, 0.15625, ((0, 8), (1, 4)))
    d_out = normal_values(streams_of[6], (TOKENS, D), 0.25, 1.5, ((0, 4), (1, 8)))
    return dict(tokens=tokens, route=route, gate_prob=gate_prob, w_gate=w_gate, w_up=w_up, w_down=w_down, d_out=d_out)


def rounded(value):
    return lax.optimization_barrier(value.astype(jnp.bfloat16)).astype(jnp.float32)


def reference(tokens, route, gate_prob, w_gate, w_up, w_down, d_out):
    pieces = N_OWNER // EXPERTS
    width = FF // pieces
    chosen = route[:, 0]
    dy_full = d_out.astype(jnp.float32)
    out_sum = jnp.zeros((TOKENS, D), jnp.float32)
    input_sum = jnp.zeros((TOKENS, D), jnp.float32)
    grad_gate = jnp.zeros((TOKENS,), jnp.float32)
    gate_blocks = []
    up_blocks = []
    down_blocks = []
    for expert in range(EXPERTS):
        member = chosen == expert
        row_weights = jnp.where(member, gate_prob, jnp.float32(0.0))
        gate_block = w_gate[:, expert * FF:(expert + 1) * FF]
        up_block = w_up[:, expert * FF:(expert + 1) * FF]
        down_block = w_down[expert * FF:(expert + 1) * FF, :]
        gate_pre = jnp.dot(tokens, gate_block, preferred_element_type=jnp.float32)
        up_pre = jnp.dot(tokens, up_block, preferred_element_type=jnp.float32)
        sigma = jax.nn.sigmoid(gate_pre)
        active = gate_pre * sigma
        hidden = jnp.where(member[:, None], active * up_pre, jnp.float32(0.0)).astype(jnp.bfloat16)
        expert_out = jnp.dot(hidden, down_block, preferred_element_type=jnp.float32)
        grad_gate = grad_gate + jnp.where(member, jnp.sum(dy_full * expert_out, axis=1), jnp.float32(0.0))
        d_expert = (row_weights[:, None] * dy_full).astype(jnp.bfloat16)
        d_hidden = jnp.dot(d_expert, down_block.T, preferred_element_type=jnp.float32)
        d_gate_pre = (d_hidden * up_pre * sigma * (1.0 + gate_pre * (1.0 - sigma))).astype(jnp.bfloat16)
        d_up_pre = (d_hidden * active).astype(jnp.bfloat16)
        for portion in range(pieces):
            start_col = portion * width
            end_col = start_col + width
            piece_out = jnp.dot(hidden[:, start_col:end_col], down_block[start_col:end_col, :], preferred_element_type=jnp.float32)
            out_sum = out_sum + rounded(row_weights[:, None] * piece_out)
            piece_input = jnp.dot(d_gate_pre[:, start_col:end_col], gate_block[:, start_col:end_col].T, preferred_element_type=jnp.float32)
            piece_input = piece_input + jnp.dot(d_up_pre[:, start_col:end_col], up_block[:, start_col:end_col].T, preferred_element_type=jnp.float32)
            input_sum = input_sum + rounded(piece_input)
        gate_grad = jnp.zeros((D, FF), jnp.float32)
        up_grad = jnp.zeros((D, FF), jnp.float32)
        down_grad = jnp.zeros((FF, D), jnp.float32)
        for group in range(N_DP):
            first_row = group * TOK_GRP
            last_row = first_row + TOK_GRP
            block_tokens = tokens[first_row:last_row].T
            gate_grad = gate_grad + rounded(jnp.dot(block_tokens, d_gate_pre[first_row:last_row], preferred_element_type=jnp.float32))
            up_grad = up_grad + rounded(jnp.dot(block_tokens, d_up_pre[first_row:last_row], preferred_element_type=jnp.float32))
            down_grad = down_grad + rounded(jnp.dot(hidden[first_row:last_row].T, d_expert[first_row:last_row], preferred_element_type=jnp.float32))
        gate_blocks.append(gate_grad)
        up_blocks.append(up_grad)
        down_blocks.append(down_grad)
    mixed = out_sum.astype(jnp.bfloat16)
    grad_tokens = input_sum.astype(jnp.bfloat16)
    grad_w_gate = jnp.concatenate(gate_blocks, axis=1)
    grad_w_up = jnp.concatenate(up_blocks, axis=1)
    grad_w_down = jnp.concatenate(down_blocks, axis=0)
    return (mixed, grad_tokens, grad_gate, grad_w_gate, grad_w_up, grad_w_down)
```

```python
import jax
import jax.numpy as jnp
from jax import lax
from jax.sharding import PartitionSpec as P

EXPERTS = 4
BF = jnp.bfloat16
F32 = jnp.float32


def contract_rows(left, right):
    return lax.dot_general(
        left, right, (((0,), (0,)), ((), ())), preferred_element_type=jnp.float32
    )


def contract_cols(left, right):
    return lax.dot_general(
        left, right, (((1,), (1,)), ((), ())), preferred_element_type=jnp.float32
    )


def dot(left, right):
    return jnp.dot(left, right, preferred_element_type=jnp.float32)


def gathered(tokens, route, gate_prob, w_gate, w_up, w_down, d_out):
    row_count = tokens.shape[0]
    capacity = 3 * row_count // 4
    pieces = lax.axis_size("owner") // EXPERTS
    expert = lax.axis_index("owner") // pieces
    full_gate, full_up, full_down = (
        lax.all_gather(w_gate, "dp", axis=0, tiled=True),
        lax.all_gather(w_up, "dp", axis=0, tiled=True),
        lax.all_gather(w_down, "dp", axis=1, tiled=True),
    )
    selected = route[:, 0] == expert
    slot_index = jnp.cumsum(selected.astype(jnp.int32)) - 1
    safe_index = jnp.maximum(slot_index, 0)
    slot_ids = jnp.arange(capacity, dtype=jnp.int32)
    one_hot = jnp.logical_and(slot_index[None, :] == slot_ids[:, None], selected[None, :])
    dispatch = one_hot.astype(jnp.bfloat16)
    slot_tokens = dot(dispatch, tokens).astype(jnp.bfloat16)
    slot_probs = jnp.sum(jnp.where(one_hot, gate_prob[None, :], jnp.float32(0.0)), axis=1)
    row_weights = jnp.where(selected, gate_prob, jnp.float32(0.0))
    gate_pre = dot(slot_tokens, full_gate)
    up_pre = dot(slot_tokens, full_up)
    sigma = jax.nn.sigmoid(gate_pre)
    active = gate_pre * sigma
    hidden = (active * up_pre).astype(jnp.bfloat16)
    expert_out = dot(hidden, full_down)
    row_terms = jnp.take(expert_out, safe_index, axis=0) * row_weights[:, None]
    mixed = lax.psum_scatter(
        row_terms.astype(jnp.bfloat16), "owner", scatter_dimension=1, tiled=True
    )
    d_full = lax.all_gather(d_out, "owner", axis=1, tiled=True)
    slot_cotangent = dot(dispatch, d_full)
    slot_router = jnp.sum(slot_cotangent * expert_out, axis=1)
    router_terms = jnp.where(selected, jnp.take(slot_router, safe_index), jnp.float32(0.0))
    grad_gate = lax.psum(router_terms, "owner")
    d_expert = (slot_probs[:, None] * slot_cotangent).astype(jnp.bfloat16)
    d_hidden = contract_cols(d_expert, full_down)
    d_gate_pre = (d_hidden * up_pre * sigma * (1.0 + gate_pre * (1.0 - sigma))).astype(jnp.bfloat16)
    d_up_pre = (d_hidden * active).astype(jnp.bfloat16)
    slot_input = contract_cols(d_gate_pre, full_gate) + contract_cols(d_up_pre, full_up)
    input_terms = jnp.where(
        selected[:, None], jnp.take(slot_input, safe_index, axis=0), jnp.float32(0.0)
    )
    grad_tokens = lax.psum_scatter(
        input_terms.astype(jnp.bfloat16), "owner", scatter_dimension=1, tiled=True
    )
    gate_term = contract_rows(slot_tokens, d_gate_pre)
    up_term = contract_rows(slot_tokens, d_up_pre)
    down_term = contract_rows(hidden, d_expert)
    grad_w_gate, grad_w_up, grad_w_down = (
        lax.psum_scatter(
            gate_term.astype(jnp.bfloat16), "dp", scatter_dimension=0, tiled=True
        ).astype(jnp.float32),
        lax.psum_scatter(
            up_term.astype(jnp.bfloat16), "dp", scatter_dimension=0, tiled=True
        ).astype(jnp.float32),
        lax.psum_scatter(
            down_term.astype(jnp.bfloat16), "dp", scatter_dimension=1, tiled=True
        ).astype(jnp.float32),
    )
    return (mixed, grad_tokens, grad_gate, grad_w_gate, grad_w_up, grad_w_down)


def swap(value, axis, bit):
    pairs = [(i, i ^ bit) for i in range(lax.axis_size(axis))]
    return lax.ppermute(value, axis, pairs)


def by_core(value):
    return swap(value, "dp", 1)


def by_y(value):
    return swap(value, "dp", 2)


def by_x(value):
    return swap(value, "owner", 1)


def by_z(value, step):
    return swap(value, "owner", 2 * step)


def take_cols(value, index, width):
    return lax.dynamic_slice_in_dim(value, index * width, width, axis=1)


def exchanged(tokens, route, gate_prob, w_gate, w_up, w_down, d_out):
    rows, width = tokens.shape
    capacity = 3 * rows // 4
    quarter = width // 4
    part = d_out.shape[1]
    d = lax.axis_index("dp")
    owner = lax.axis_index("owner")
    z, x = owner // 2, owner % 2
    turn = d ^ z

    relative = route[:, 0] ^ z
    member = relative[None, :] == jnp.arange(EXPERTS, dtype=jnp.int32)[:, None]
    rank = jnp.cumsum(member.astype(jnp.int32), axis=1) - 1
    slot = jnp.sum(jnp.where(member, rank, 0), axis=0) + relative * capacity
    hot = slot[None, :] == jnp.arange(EXPERTS * capacity, dtype=jnp.int32)[:, None]
    place = hot.astype(BF)
    own_hot, own_place = hot[:capacity], place[:capacity]
    prob_own = jnp.sum(jnp.where(own_hot, gate_prob[None, :], F32(0.0)), axis=1)[:, None]
    prob_rem = by_y(prob_own)

    cot = dot(place, d_out).astype(BF).reshape(EXPERTS, capacity, part)
    cot_s = jnp.stack([cot[0]] + [by_z(cot[s], s) for s in (1, 2, 3)])

    def x_cols(k):
        return take_cols(tokens, d ^ k, quarter)

    x_send = dot(own_place, jnp.concatenate([x_cols(2), x_cols(3)], axis=1)).astype(BF)
    x_rem = by_y(x_send)
    x_own = dot(own_place, jnp.concatenate([x_cols(0), x_cols(1)], axis=1)).astype(BF)

    core_gate, core_up, core_down = by_core(w_gate), by_core(w_up), by_core(w_down)
    half_gate = jnp.concatenate([w_gate, core_gate], axis=0)
    half_up = jnp.concatenate([w_up, core_up], axis=0)

    def down_of(j):
        return jnp.concatenate([take_cols(w_down, j, part), take_cols(core_down, j, part)], axis=1)

    def rows_of(own, core, j):
        def cut(value):
            return lax.dynamic_slice_in_dim(value, j * part, part, axis=0)

        return jnp.concatenate([cut(own), cut(core)], axis=0)

    down_mine, down_other = down_of(x), down_of(1 - x)
    gate_mine, gate_other = (rows_of(w_gate, core_gate, j) for j in (x, 1 - x))
    up_mine, up_other = (rows_of(w_up, core_up, j) for j in (x, 1 - x))

    def projected(x_rows):
        return dot(x_rows, half_gate), dot(x_rows, half_up)

    def full_sum(own, rem):
        own_bf, rem_bf = own.astype(BF), rem.astype(BF)
        from_own, from_rem = by_y(own_bf), by_y(rem_bf)
        return own + from_rem.astype(F32), rem + from_own.astype(F32)

    def full_pair(own, rem):
        own_bf = jnp.concatenate([v.astype(BF) for v in own], axis=1)
        rem_bf = jnp.concatenate([v.astype(BF) for v in rem], axis=1)
        n = own[0].shape[1]
        from_own, from_rem = by_y(own_bf).astype(F32), by_y(rem_bf).astype(F32)
        return (
            (own[0] + from_rem[:, :n], own[1] + from_rem[:, n:]),
            (rem[0] + from_own[:, :n], rem[1] + from_own[:, n:]),
        )

    pre_own, pre_rem = full_pair(projected(x_own), projected(x_rem))

    def cot_at(k):
        return lax.dynamic_index_in_dim(cot_s, turn ^ k, axis=0, keepdims=False)

    cot_own = jnp.concatenate([cot_at(0), cot_at(1)], axis=1)
    cot_rem = by_y(jnp.concatenate([cot_at(2), cot_at(3)], axis=1))

    cot_own_other, cot_rem_other = by_x(cot_own), by_x(cot_rem)

    def back_of(mine, other):
        return contract_cols(mine, down_mine) + contract_cols(other, down_other)

    back_own, back_rem = full_sum(
        back_of(cot_own, cot_own_other), back_of(cot_rem, cot_rem_other)
    )

    def pointwise(pre, back, prob):
        gate_pre, up_pre = pre
        sigma = jax.nn.sigmoid(gate_pre)
        active = gate_pre * sigma
        hidden = active * up_pre
        scaled = (prob * hidden).astype(BF)
        d_hidden = prob * back
        d_gate = (d_hidden * up_pre * sigma * (1.0 + gate_pre * (1.0 - sigma))).astype(BF)
        d_up = (d_hidden * active).astype(BF)
        return hidden, scaled, d_gate, d_up

    hidden_own, scaled_own, d_gate_own, d_up_own = pointwise(pre_own, back_own, prob_own)
    _, scaled_rem, d_gate_rem, d_up_rem = pointwise(pre_rem, back_rem, prob_rem)

    router = jnp.sum(hidden_own * back_own, axis=1)
    grad_gate = jnp.sum(jnp.where(own_hot, router[:, None], F32(0.0)), axis=0)
    grad_gate = grad_gate + by_x(grad_gate)
    grad_gate = grad_gate + by_z(grad_gate, 1)
    grad_gate = grad_gate + by_z(grad_gate, 2)

    def over_x(mine, other):
        return (mine + by_x(other.astype(BF)).astype(F32)).astype(BF)

    def returned(own, rem):
        far = by_y(over_x(*rem))
        near = over_x(*own)
        blocks = jnp.stack([near[:, :part], near[:, part:], far[:, :part], far[:, part:]])
        sent = [lax.dynamic_index_in_dim(blocks, turn ^ s, axis=0, keepdims=False) for s in range(4)]
        got = jnp.concatenate([sent[0]] + [by_z(sent[s], s) for s in (1, 2, 3)], axis=0)
        return contract_rows(place, got).astype(BF)

    def output(scaled):
        return dot(scaled, down_mine), dot(scaled, down_other)

    def d_input(d_gate, d_up):
        return (
            contract_cols(d_gate, gate_mine) + contract_cols(d_up, up_mine),
            contract_cols(d_gate, gate_other) + contract_cols(d_up, up_other),
        )

    mixed = returned(output(scaled_own), output(scaled_rem))
    grad_tokens = returned(d_input(d_gate_own, d_up_own), d_input(d_gate_rem, d_up_rem))

    x_all = jnp.concatenate([x_own, x_rem], axis=0)
    mine_all = jnp.concatenate([cot_own, cot_rem], axis=0)
    other_all = jnp.concatenate([cot_own_other, cot_rem_other], axis=0)
    d_gate_all = jnp.concatenate([d_gate_own, d_gate_rem], axis=0)
    d_up_all = jnp.concatenate([d_up_own, d_up_rem], axis=0)
    scaled_all = jnp.concatenate([scaled_own, scaled_rem], axis=0)

    def in_chip(keep, send):
        return keep + by_core(send.astype(BF)).astype(F32)

    x_keep, x_give = x_all[:, :quarter], x_all[:, quarter:]
    grad_w_gate = in_chip(contract_rows(x_keep, d_gate_all), contract_rows(x_give, d_gate_all))
    grad_w_up = in_chip(contract_rows(x_keep, d_up_all), contract_rows(x_give, d_up_all))
    down_keep = jnp.concatenate([mine_all[:, :part], other_all[:, :part]], axis=1)
    down_give = jnp.concatenate([mine_all[:, part:], other_all[:, part:]], axis=1)
    grad_down = in_chip(contract_rows(scaled_all, down_keep), contract_rows(scaled_all, down_give))
    turned = jnp.concatenate([grad_down[:, part:], grad_down[:, :part]], axis=1)
    grad_w_down = jnp.where(x == 0, grad_down, turned)
    return (mixed, grad_tokens, grad_gate, grad_w_gate, grad_w_up, grad_w_down)


def solution(mesh):
    in_specs = (
        P("dp", None),
        P("dp", None),
        P("dp"),
        P("dp", "owner"),
        P("dp", "owner"),
        P("owner", "dp"),
        P("dp", "owner"),
    )
    out_specs = (
        P("dp", "owner"),
        P("dp", "owner"),
        P("dp"),
        P("dp", "owner"),
        P("dp", "owner"),
        P("owner", "dp"),
    )
    local = exchanged if (mesh.shape["dp"], mesh.shape["owner"]) == (4, 8) else gathered
    return jax.shard_map(local, mesh=mesh, in_specs=in_specs, out_specs=out_specs, check_vma=False)
```

```python
import jax
import jax.numpy as jnp
from jax import lax
from jax.sharding import PartitionSpec as P

EXPERTS = 4
XDEPTH = 1
BF = jnp.bfloat16
F32 = jnp.float32


def contract_rows(left, right):
    return lax.dot_general(
        left, right, (((0,), (0,)), ((), ())), preferred_element_type=jnp.float32
    )


def contract_cols(left, right):
    return lax.dot_general(
        left, right, (((1,), (1,)), ((), ())), preferred_element_type=jnp.float32
    )


def dot(left, right):
    return jnp.dot(left, right, preferred_element_type=jnp.float32)


def gathered(tokens, route, gate_prob, w_gate, w_up, w_down, d_out):
    row_count = tokens.shape[0]
    capacity = 3 * row_count // 4
    pieces = lax.axis_size("owner") // EXPERTS
    expert = lax.axis_index("owner") // pieces
    full_gate, full_up, full_down = (
        lax.all_gather(w_gate, "dp", axis=0, tiled=True),
        lax.all_gather(w_up, "dp", axis=0, tiled=True),
        lax.all_gather(w_down, "dp", axis=1, tiled=True),
    )
    selected = route[:, 0] == expert
    slot_index = jnp.cumsum(selected.astype(jnp.int32)) - 1
    safe_index = jnp.maximum(slot_index, 0)
    slot_ids = jnp.arange(capacity, dtype=jnp.int32)
    one_hot = jnp.logical_and(slot_index[None, :] == slot_ids[:, None], selected[None, :])
    dispatch = one_hot.astype(jnp.bfloat16)
    slot_tokens = dot(dispatch, tokens).astype(jnp.bfloat16)
    slot_probs = jnp.sum(jnp.where(one_hot, gate_prob[None, :], jnp.float32(0.0)), axis=1)
    row_weights = jnp.where(selected, gate_prob, jnp.float32(0.0))
    gate_pre = dot(slot_tokens, full_gate)
    up_pre = dot(slot_tokens, full_up)
    sigma = jax.nn.sigmoid(gate_pre)
    active = gate_pre * sigma
    hidden = (active * up_pre).astype(jnp.bfloat16)
    expert_out = dot(hidden, full_down)
    row_terms = jnp.take(expert_out, safe_index, axis=0) * row_weights[:, None]
    mixed = lax.psum_scatter(
        row_terms.astype(jnp.bfloat16), "owner", scatter_dimension=1, tiled=True
    )
    d_full = lax.all_gather(d_out, "owner", axis=1, tiled=True)
    slot_cotangent = dot(dispatch, d_full)
    slot_router = jnp.sum(slot_cotangent * expert_out, axis=1)
    router_terms = jnp.where(selected, jnp.take(slot_router, safe_index), jnp.float32(0.0))
    grad_gate = lax.psum(router_terms, "owner")
    d_expert = (slot_probs[:, None] * slot_cotangent).astype(jnp.bfloat16)
    d_hidden = contract_cols(d_expert, full_down)
    d_gate_pre = (d_hidden * up_pre * sigma * (1.0 + gate_pre * (1.0 - sigma))).astype(jnp.bfloat16)
    d_up_pre = (d_hidden * active).astype(jnp.bfloat16)
    slot_input = contract_cols(d_gate_pre, full_gate) + contract_cols(d_up_pre, full_up)
    input_terms = jnp.where(
        selected[:, None], jnp.take(slot_input, safe_index, axis=0), jnp.float32(0.0)
    )
    grad_tokens = lax.psum_scatter(
        input_terms.astype(jnp.bfloat16), "owner", scatter_dimension=1, tiled=True
    )
    gate_term = contract_rows(slot_tokens, d_gate_pre)
    up_term = contract_rows(slot_tokens, d_up_pre)
    down_term = contract_rows(hidden, d_expert)
    grad_w_gate, grad_w_up, grad_w_down = (
        lax.psum_scatter(
            gate_term.astype(jnp.bfloat16), "dp", scatter_dimension=0, tiled=True
        ).astype(jnp.float32),
        lax.psum_scatter(
            up_term.astype(jnp.bfloat16), "dp", scatter_dimension=0, tiled=True
        ).astype(jnp.float32),
        lax.psum_scatter(
            down_term.astype(jnp.bfloat16), "dp", scatter_dimension=1, tiled=True
        ).astype(jnp.float32),
    )
    return (mixed, grad_tokens, grad_gate, grad_w_gate, grad_w_up, grad_w_down)


def swap(value, axis, bit):
    pairs = [(i, i ^ bit) for i in range(lax.axis_size(axis))]
    return lax.ppermute(value, axis, pairs)


def after(value, *others):
    return lax.optimization_barrier((value,) + others)[0]


class Line:
    def __init__(self, axis, depth):
        self.axis, self.depth, self.done = axis, depth, []

    def __call__(self, value, bit):
        if len(self.done) >= self.depth:
            value = after(value, self.done[-self.depth])
        self.done.append(swap(value, self.axis, bit))
        return self.done[-1]


def take_cols(value, index, width):
    return lax.dynamic_slice_in_dim(value, index * width, width, axis=1)


def exchanged(tokens, route, gate_prob, w_gate, w_up, w_down, d_out):
    rows, width = tokens.shape
    capacity = 3 * rows // 4
    quarter = width // 4
    part = d_out.shape[1]
    d = lax.axis_index("dp")
    owner = lax.axis_index("owner")
    z, x = owner // 2, owner % 2
    y_line, x_line = Line("dp", 1), Line("owner", XDEPTH)

    def by_core(value):
        return swap(value, "dp", 1)

    def by_y(value):
        return y_line(value, 2)

    def by_x(value):
        return x_line(value, 1)

    def over_z(blocks):
        groups = [[2 * i + j for i in range(EXPERTS)] for j in range(2)]
        got = lax.all_to_all(blocks, "owner", 0, 0, tiled=True, axis_index_groups=groups)
        return got.reshape(EXPERTS, -1, part)

    experts = jnp.arange(EXPERTS, dtype=jnp.int32)[:, None]
    member = route.T == experts
    rank = jnp.cumsum(member.astype(jnp.int32), axis=1) - 1
    rank = jnp.sum(jnp.where(member, rank, 0), axis=0)
    own_slot = jnp.where(route[:, 0] == z, rank, -1)
    own_place = (own_slot[None, :] == jnp.arange(capacity, dtype=jnp.int32)[:, None]).astype(BF)
    slot = rank + route[:, 0] * capacity
    hot = slot[None, :] == jnp.arange(EXPERTS * capacity, dtype=jnp.int32)[:, None]
    place = hot.astype(BF)

    def x_cols(k):
        return take_cols(tokens, d ^ k, quarter)

    x_got = by_y(dot(own_place, x_cols(2 + x)).astype(BF))
    x_own = [dot(own_place, x_cols(k)).astype(BF) for k in (0, 1)]

    d_expert = (gate_prob[:, None] * d_out.astype(F32)).astype(BF)
    cot_got = over_z(dot(place, d_expert).astype(BF))

    core_gate, core_up, core_down = by_core(w_gate), by_core(w_up), by_core(w_down)

    def projected(x_rows):
        return (
            dot(x_rows[0], w_gate) + dot(x_rows[1], core_gate),
            dot(x_rows[0], w_up) + dot(x_rows[1], core_up),
        )

    def joined(pair):
        return jnp.concatenate([v.astype(BF) for v in pair], axis=1)

    part_own = projected(x_own)
    sent_own = joined(part_own)
    far_rem = by_y(sent_own)
    x_other = by_x(x_got)
    x_rem = [jnp.where(x == 0, x_got, x_other), jnp.where(x == 0, x_other, x_got)]
    part_rem = projected(x_rem)
    sent_rem = joined(part_rem)
    far_own = by_y(sent_rem)

    def down_of(j):
        return jnp.concatenate([take_cols(own_down, j, part), take_cols(core_down, j, part)], axis=1)

    def rows_of(own, core, j):
        def cut(value):
            return lax.dynamic_slice_in_dim(value, j * part, part, axis=0)

        return jnp.concatenate([cut(own), cut(core)], axis=0)

    own_gate, own_up, own_down, core_gate, core_up, core_down, _ = lax.optimization_barrier(
        (w_gate, w_up, w_down, core_gate, core_up, core_down, sent_own)
    )
    down_mine, down_other = down_of(x), down_of(1 - x)
    gate_mine, gate_other = (rows_of(own_gate, core_gate, j) for j in (x, 1 - x))
    up_mine, up_other = (rows_of(own_up, core_up, j) for j in (x, 1 - x))

    def cot_at(k):
        return lax.dynamic_index_in_dim(cot_got, d ^ k, axis=0, keepdims=False)

    cot_rem = by_y(jnp.concatenate([cot_at(2), cot_at(3)], axis=1))
    cot_own = jnp.concatenate([cot_at(0), cot_at(1)], axis=1)
    cot_own_other = by_x(cot_own)

    def back_of(mine, other):
        return contract_cols(mine, down_mine) + contract_cols(other, down_other)

    def forward(pair, far):
        n = pair[0].shape[1]
        gate_pre = pair[0] + far[:, :n].astype(F32)
        up_pre = pair[1] + far[:, n:].astype(F32)
        sigma = jax.nn.sigmoid(gate_pre)
        active = gate_pre * sigma
        return gate_pre, up_pre, sigma, active, (active * up_pre).astype(BF)

    def backward(pre, back, far):
        gate_pre, up_pre, sigma, active, hidden = pre
        d_hidden = back + far.astype(F32)
        d_gate = (d_hidden * up_pre * sigma * (1.0 + gate_pre * (1.0 - sigma))).astype(BF)
        d_up = (d_hidden * active).astype(BF)
        return d_gate, d_up, jnp.sum(hidden.astype(F32) * d_hidden, axis=1)

    pre_own, pre_rem = forward(part_own, far_own), forward(part_rem, far_rem)
    hidden_own, hidden_rem = pre_own[-1], pre_rem[-1]

    def added(mine, got):
        return (mine + got.astype(F32)).astype(BF)

    def output(hidden):
        return dot(hidden, down_mine), dot(hidden, down_other)

    def d_input(d_gate, d_up):
        return (
            contract_cols(d_gate, gate_mine) + contract_cols(d_up, up_mine),
            contract_cols(d_gate, gate_other) + contract_cols(d_up, up_other),
        )

    def plane_blocks(near, far, note=None):
        blocks = jnp.stack([near[:, :part], near[:, part:], far[:, :part], far[:, part:]])
        sent = [lax.dynamic_index_in_dim(blocks, d ^ i, axis=0, keepdims=False) for i in range(EXPERTS)]
        if note is not None:
            sent = [v for value in sent for v in (value, note)]
        return jnp.concatenate(sent, axis=0)

    def placed(got):
        return contract_rows(place, got[:, :capacity].reshape(EXPERTS * capacity, part))

    def noted(value):
        first = value.astype(BF)
        second = (value - first.astype(F32)).astype(BF)
        third = (value - first.astype(F32) - second.astype(F32)).astype(BF)
        lines = jnp.stack([first, second, third])
        return jnp.pad(lines, ((0, 13), (0, part - value.shape[0])))

    def read_note(lines):
        return jnp.sum(lines[:3, :capacity].astype(F32), axis=0)

    back_own = back_of(cot_own, cot_own_other)
    back_far_rem = by_y(back_own.astype(BF))

    mine, other = output(hidden_rem)
    out_got = by_x(other.astype(BF))
    cot_rem_other = by_x(cot_rem)
    out_rem = added(mine, out_got)
    out_far = by_y(out_rem)
    out_mine, out_other = output(hidden_own)
    out_near = added(out_mine, by_x(out_other.astype(BF)))

    back_rem = back_of(cot_rem, cot_rem_other)
    back_far_own = by_y(after(back_rem.astype(BF), out_near))
    out_sent = plane_blocks(out_near, out_far)
    out_blocks = over_z(out_sent)
    back_far_rem, back_far_own, _ = lax.optimization_barrier((back_far_rem, back_far_own, out_sent))

    d_gate_rem, d_up_rem, _ = backward(pre_rem, back_rem, back_far_rem)
    d_gate_own, d_up_own, router = backward(pre_own, back_own, back_far_own)
    mine, other = d_input(d_gate_rem, d_up_rem)
    in_far = by_y(added(mine, by_x(other.astype(BF))))
    mine, other = d_input(d_gate_own, d_up_own)
    wide = jnp.pad(noted(router), ((0, 0), (0, other.shape[1] - part)))
    in_sent = jnp.concatenate([other.astype(BF), wide], axis=0)
    in_got = by_x(in_sent)
    in_near = added(mine, in_got[:capacity])
    in_blocks = over_z(
        plane_blocks(in_near, in_far, noted(router + read_note(in_got[capacity:])))
    )

    notes = jnp.concatenate([read_note(v) for v in in_blocks[:, capacity:]])
    grad_gate = jnp.sum(jnp.where(hot, notes[:, None], F32(0.0)), axis=0) / gate_prob
    mixed = (gate_prob[:, None] * placed(out_blocks)).astype(BF)
    grad_tokens = placed(in_blocks).astype(BF)

    d_gate_own, d_gate_rem, d_up_own, d_up_rem, _ = lax.optimization_barrier(
        (d_gate_own, d_gate_rem, d_up_own, d_up_rem, in_sent)
    )
    hidden_own, hidden_rem, _ = lax.optimization_barrier((hidden_own, hidden_rem, in_sent))
    x_keep, x_give = (jnp.concatenate([own, rem], axis=0) for own, rem in zip(x_own, x_rem))
    mine_all = jnp.concatenate([cot_own, cot_rem], axis=0)
    other_all = jnp.concatenate([cot_own_other, cot_rem_other], axis=0)
    d_gate_all = jnp.concatenate([d_gate_own, d_gate_rem], axis=0)
    d_up_all = jnp.concatenate([d_up_own, d_up_rem], axis=0)
    hidden_all = jnp.concatenate([hidden_own, hidden_rem], axis=0)

    def in_chip(keep, give):
        return keep + by_core(give.astype(BF)).astype(F32)

    grad_w_gate = in_chip(contract_rows(x_keep, d_gate_all), contract_rows(x_give, d_gate_all))
    grad_w_up = in_chip(contract_rows(x_keep, d_up_all), contract_rows(x_give, d_up_all))
    down_keep = jnp.concatenate([mine_all[:, :part], other_all[:, :part]], axis=1)
    down_give = jnp.concatenate([mine_all[:, part:], other_all[:, part:]], axis=1)
    grad_down = in_chip(contract_rows(hidden_all, down_keep), contract_rows(hidden_all, down_give))
    turned = jnp.concatenate([grad_down[:, part:], grad_down[:, :part]], axis=1)
    grad_w_down = jnp.where(x == 0, grad_down, turned)
    return (mixed, grad_tokens, grad_gate, grad_w_gate, grad_w_up, grad_w_down)


def solution(mesh):
    in_specs = (
        P("dp", None),
        P("dp", None),
        P("dp"),
        P("dp", "owner"),
        P("dp", "owner"),
        P("owner", "dp"),
        P("dp", "owner"),
    )
    out_specs = (
        P("dp", "owner"),
        P("dp", "owner"),
        P("dp"),
        P("dp", "owner"),
        P("dp", "owner"),
        P("owner", "dp"),
    )
    local = exchanged if (mesh.shape["dp"], mesh.shape["owner"]) == (4, 8) else gathered
    return jax.shard_map(local, mesh=mesh, in_specs=in_specs, out_specs=out_specs, check_vma=False)
```

```python
import jax
import jax.numpy as jnp
from jax import lax
from jax.experimental import pallas as pl
from jax.experimental.pallas import tpu as pltpu
from jax.sharding import PartitionSpec as P

EXPERTS = 4
XDEPTH = 1
COST = 1024
OWN_COST = 20 * 10**9
BF = jnp.bfloat16
F32 = jnp.float32


def contract_rows(left, right):
    return lax.dot_general(
        left, right, (((0,), (0,)), ((), ())), preferred_element_type=jnp.float32
    )


def contract_cols(left, right):
    return lax.dot_general(
        left, right, (((1,), (1,)), ((), ())), preferred_element_type=jnp.float32
    )


def dot(left, right):
    return jnp.dot(left, right, preferred_element_type=jnp.float32)


def gathered(tokens, route, gate_prob, w_gate, w_up, w_down, d_out):
    row_count = tokens.shape[0]
    capacity = 3 * row_count // 4
    pieces = lax.axis_size("owner") // EXPERTS
    expert = lax.axis_index("owner") // pieces
    full_gate, full_up, full_down = (
        lax.all_gather(w_gate, "dp", axis=0, tiled=True),
        lax.all_gather(w_up, "dp", axis=0, tiled=True),
        lax.all_gather(w_down, "dp", axis=1, tiled=True),
    )
    selected = route[:, 0] == expert
    slot_index = jnp.cumsum(selected.astype(jnp.int32)) - 1
    safe_index = jnp.maximum(slot_index, 0)
    slot_ids = jnp.arange(capacity, dtype=jnp.int32)
    one_hot = jnp.logical_and(slot_index[None, :] == slot_ids[:, None], selected[None, :])
    dispatch = one_hot.astype(jnp.bfloat16)
    slot_tokens = dot(dispatch, tokens).astype(jnp.bfloat16)
    slot_probs = jnp.sum(jnp.where(one_hot, gate_prob[None, :], jnp.float32(0.0)), axis=1)
    row_weights = jnp.where(selected, gate_prob, jnp.float32(0.0))
    gate_pre = dot(slot_tokens, full_gate)
    up_pre = dot(slot_tokens, full_up)
    sigma = jax.nn.sigmoid(gate_pre)
    active = gate_pre * sigma
    hidden = (active * up_pre).astype(jnp.bfloat16)
    expert_out = dot(hidden, full_down)
    row_terms = jnp.take(expert_out, safe_index, axis=0) * row_weights[:, None]
    mixed = lax.psum_scatter(
        row_terms.astype(jnp.bfloat16), "owner", scatter_dimension=1, tiled=True
    )
    d_full = lax.all_gather(d_out, "owner", axis=1, tiled=True)
    slot_cotangent = dot(dispatch, d_full)
    slot_router = jnp.sum(slot_cotangent * expert_out, axis=1)
    router_terms = jnp.where(selected, jnp.take(slot_router, safe_index), jnp.float32(0.0))
    grad_gate = lax.psum(router_terms, "owner")
    d_expert = (slot_probs[:, None] * slot_cotangent).astype(jnp.bfloat16)
    d_hidden = contract_cols(d_expert, full_down)
    d_gate_pre = (d_hidden * up_pre * sigma * (1.0 + gate_pre * (1.0 - sigma))).astype(jnp.bfloat16)
    d_up_pre = (d_hidden * active).astype(jnp.bfloat16)
    slot_input = contract_cols(d_gate_pre, full_gate) + contract_cols(d_up_pre, full_up)
    input_terms = jnp.where(
        selected[:, None], jnp.take(slot_input, safe_index, axis=0), jnp.float32(0.0)
    )
    grad_tokens = lax.psum_scatter(
        input_terms.astype(jnp.bfloat16), "owner", scatter_dimension=1, tiled=True
    )
    gate_term = contract_rows(slot_tokens, d_gate_pre)
    up_term = contract_rows(slot_tokens, d_up_pre)
    down_term = contract_rows(hidden, d_expert)
    grad_w_gate, grad_w_up, grad_w_down = (
        lax.psum_scatter(
            gate_term.astype(jnp.bfloat16), "dp", scatter_dimension=0, tiled=True
        ).astype(jnp.float32),
        lax.psum_scatter(
            up_term.astype(jnp.bfloat16), "dp", scatter_dimension=0, tiled=True
        ).astype(jnp.float32),
        lax.psum_scatter(
            down_term.astype(jnp.bfloat16), "dp", scatter_dimension=1, tiled=True
        ).astype(jnp.float32),
    )
    return (mixed, grad_tokens, grad_gate, grad_w_gate, grad_w_up, grad_w_down)


def swap(value, axis, bit):
    pairs = [(i, i ^ bit) for i in range(lax.axis_size(axis))]
    return lax.ppermute(value, axis, pairs)


def after(value, *others):
    return lax.optimization_barrier((value,) + others)[0]


class Line:
    def __init__(self, axis, depth):
        self.axis, self.depth, self.done = axis, depth, []

    def __call__(self, value, bit):
        if len(self.done) >= self.depth:
            value = after(value, self.done[-self.depth])
        self.done.append(swap(value, self.axis, bit))
        return self.done[-1]


def on_core(body, outs, *args, cost=COST):
    vmem = pl.BlockSpec(memory_space=pltpu.VMEM)
    return pl.pallas_call(
        body,
        out_shape=[jax.ShapeDtypeStruct(shape, kind) for shape, kind in outs],
        in_specs=[pl.BlockSpec(memory_space=pltpu.SMEM)] + [vmem] * (len(args) - 1),
        out_specs=[vmem] * len(outs),
        compiler_params=pltpu.CompilerParams(vmem_limit_bytes=32 * 1024 * 1024),
        cost_estimate=pl.CostEstimate(flops=cost, bytes_accessed=COST, transcendentals=0),
    )(*args)


BLOCK = 256


def project_kernel(x_ref, first, second, gate, core_gate, up, core_up, out, sent):
    x = x_ref[0]
    swap_rows = x == 1
    left = jnp.where(swap_rows, second[...], first[...])
    right = jnp.where(swap_rows, first[...], second[...])
    for i, (own, core) in enumerate(((gate, core_gate), (up, core_up))):
        size = own.shape[1]
        for j in range(0, size, BLOCK):
            value = dot(left, own[:, j:j + BLOCK]) + dot(right, core[:, j:j + BLOCK])
            out[:, i * size + j:i * size + j + BLOCK] = value
            sent[:, i * size + j:i * size + j + BLOCK] = value.astype(BF)


def output_kernel(x_ref, hidden, down, core_down, mine, other):
    x = x_ref[0]
    part = down.shape[1] // 2
    for k, weight in enumerate((down, core_down)):
        for j in range(0, part, BLOCK):
            def cols(half):
                return weight[:, pl.ds(pl.multiple_of(half * part + j, BLOCK), BLOCK)]

            at = slice(k * part + j, k * part + j + BLOCK)
            mine[:, at] = dot(hidden[...], cols(x))
            other[:, at] = dot(hidden[...], cols(1 - x)).astype(BF)


def back_kernel(x_ref, mine, other, down, core_down, out, sent):
    x = x_ref[0]
    part = down.shape[1] // 2
    for j in range(0, down.shape[0], BLOCK):
        value = jnp.zeros((mine.shape[0], BLOCK), F32)
        for k, weight in enumerate((down, core_down)):
            for half, cot in ((x, mine), (1 - x, other)):
                cols = weight[j:j + BLOCK, pl.ds(pl.multiple_of(half * part, BLOCK), part)]
                value = value + contract_cols(cot[:, k * part:(k + 1) * part], cols)
        out[:, j:j + BLOCK] = value
        sent[:, j:j + BLOCK] = value.astype(BF)


def input_kernel(x_ref, d_gate, d_up, gate, core_gate, up, core_up, mine, other):
    x = x_ref[0]
    part = gate.shape[0] // 2
    for k, (gate_k, up_k) in enumerate(((gate, up), (core_gate, core_up))):
        for j in range(0, part, BLOCK):
            def value(half):
                at = pl.ds(pl.multiple_of(half * part + j, BLOCK), BLOCK)
                return contract_cols(d_gate[...], gate_k[at, :]) + contract_cols(d_up[...], up_k[at, :])

            at = slice(k * part + j, k * part + j + BLOCK)
            mine[:, at] = value(x)
            other[:, at] = value(1 - x).astype(BF)


def take_cols(value, index, width):
    return lax.dynamic_slice_in_dim(value, index * width, width, axis=1)


def exchanged(tokens, route, gate_prob, w_gate, w_up, w_down, d_out):
    rows, width = tokens.shape
    capacity = 3 * rows // 4
    quarter = width // 4
    part = d_out.shape[1]
    d = lax.axis_index("dp")
    owner = lax.axis_index("owner")
    z, x = owner // 2, owner % 2
    y_line, x_line = Line("dp", 1), Line("owner", XDEPTH)

    def by_core(value):
        return swap(value, "dp", 1)

    def by_y(value):
        return y_line(value, 2)

    def by_x(value):
        return x_line(value, 1)

    def over_z(blocks):
        groups = [[2 * i + j for i in range(EXPERTS)] for j in range(2)]
        got = lax.all_to_all(blocks, "owner", 0, 0, tiled=True, axis_index_groups=groups)
        return got.reshape(EXPERTS, -1, part)

    experts = jnp.arange(EXPERTS, dtype=jnp.int32)[:, None]
    member = route.T == experts
    rank = jnp.cumsum(member.astype(jnp.int32), axis=1) - 1
    rank = jnp.sum(jnp.where(member, rank, 0), axis=0)
    own_slot = jnp.where(route[:, 0] == z, rank, -1)
    own_place = (own_slot[None, :] == jnp.arange(capacity, dtype=jnp.int32)[:, None]).astype(BF)
    slot = rank + route[:, 0] * capacity
    hot = slot[None, :] == jnp.arange(EXPERTS * capacity, dtype=jnp.int32)[:, None]
    place = hot.astype(BF)

    def x_cols(k):
        return take_cols(tokens, d ^ k, quarter)

    x_sent = dot(own_place, x_cols(2 + x)).astype(BF)
    x_got = by_y(x_sent)
    x_own = [dot(own_place, x_cols(k)).astype(BF) for k in (0, 1)]

    d_expert = (gate_prob[:, None] * d_out.astype(F32)).astype(BF)
    cot_got = over_z(dot(place, after(d_expert, x_sent)).astype(BF))

    core_gate, core_up, core_down = by_core(w_gate), by_core(w_up), by_core(w_down)

    x_at, zero = jnp.reshape(x, (1,)), jnp.zeros((1,), jnp.int32)
    size = w_gate.shape[1]

    def projected(turned, first, second, cost):
        weights = (w_gate, core_gate, w_up, core_up)
        shape = (capacity, 2 * size)
        return on_core(project_kernel, ((shape, F32), (shape, BF)), turned, first, second, *weights, cost=cost)

    part_own, sent_own = projected(zero, *x_own, OWN_COST)
    far_rem = by_y(sent_own)
    x_got = after(x_got, sent_own)
    x_other = by_x(x_got)
    def cot_at(k):
        return lax.dynamic_index_in_dim(cot_got, d ^ k, axis=0, keepdims=False)

    cot_far = jnp.concatenate([cot_at(2), cot_at(3)], axis=1)
    cot_own = jnp.concatenate([cot_at(0), cot_at(1)], axis=1)
    cot_rem = by_y(cot_far)
    cot_own_other = by_x(cot_own)

    x_got, x_other, _, _ = lax.optimization_barrier((x_got, x_other, cot_far, cot_own))
    x_rem = [jnp.where(x == 0, x_got, x_other), jnp.where(x == 0, x_other, x_got)]
    part_rem, sent_rem = projected(x_at, x_got, x_other, COST)
    far_own = by_y(sent_rem)

    def back_of(mine, other):
        shape = (capacity, size)
        return on_core(back_kernel, ((shape, F32), (shape, BF)), x_at, mine, other, w_down, core_down)

    def forward(pair, far):
        pre = pair + far.astype(F32)
        gate_pre, up_pre = pre[:, :size], pre[:, size:]
        sigma = jax.nn.sigmoid(gate_pre)
        active = gate_pre * sigma
        return gate_pre, up_pre, sigma, active, (active * up_pre).astype(BF)

    def backward(pre, back, far):
        gate_pre, up_pre, sigma, active, hidden = pre
        d_hidden = back + far.astype(F32)
        d_gate = (d_hidden * up_pre * sigma * (1.0 + gate_pre * (1.0 - sigma))).astype(BF)
        d_up = (d_hidden * active).astype(BF)
        return d_gate, d_up, jnp.sum(hidden.astype(F32) * d_hidden, axis=1)

    pre_own, pre_rem = forward(part_own, far_own), forward(part_rem, far_rem)
    hidden_own, hidden_rem = pre_own[-1], pre_rem[-1]

    def added(mine, got):
        return (mine + got.astype(F32)).astype(BF)

    def output(hidden):
        shape = (capacity, 2 * part)
        return on_core(output_kernel, ((shape, F32), (shape, BF)), x_at, hidden, w_down, core_down)

    def d_input(d_gate, d_up):
        weights = (w_gate, core_gate, w_up, core_up)
        shape = (capacity, 2 * part)
        return on_core(input_kernel, ((shape, F32), (shape, BF)), x_at, d_gate, d_up, *weights)

    def plane_blocks(near, far, note=None):
        blocks = jnp.stack([near[:, :part], near[:, part:], far[:, :part], far[:, part:]])
        sent = [lax.dynamic_index_in_dim(blocks, d ^ i, axis=0, keepdims=False) for i in range(EXPERTS)]
        if note is not None:
            sent = [v for value in sent for v in (value, note)]
        return jnp.concatenate(sent, axis=0)

    def placed(got):
        return contract_rows(place, got[:, :capacity].reshape(EXPERTS * capacity, part))

    def noted(value):
        first = value.astype(BF)
        second = (value - first.astype(F32)).astype(BF)
        third = (value - first.astype(F32) - second.astype(F32)).astype(BF)
        lines = jnp.stack([first, second, third])
        return jnp.pad(lines, ((0, 13), (0, part - value.shape[0])))

    def read_note(lines):
        return jnp.sum(lines[:3, :capacity].astype(F32), axis=0)

    mine, other = output(hidden_rem)
    out_rem = added(mine, by_x(other))
    back_own, back_sent = back_of(cot_own, cot_own_other)
    back_far_rem = by_y(back_sent)
    out_far = by_y(out_rem)
    cot_rem_other = by_x(cot_rem)
    out_mine, out_other = output(hidden_own)
    out_near = added(out_mine, by_x(out_other))
    back_rem, back_sent = back_of(cot_rem, cot_rem_other)
    out_sent = plane_blocks(out_near, out_far)
    out_blocks = over_z(out_sent)
    back_far_own = by_y(after(back_sent, out_near))
    back_far_own = after(back_far_own, out_sent)

    d_gate_rem, d_up_rem, _ = backward(pre_rem, back_rem, back_far_rem)
    d_gate_own, d_up_own, router = backward(pre_own, back_own, back_far_own)
    mine, other = d_input(d_gate_rem, d_up_rem)
    in_far = by_y(added(mine, by_x(other)))
    mine, other = d_input(d_gate_own, d_up_own)
    wide = jnp.pad(noted(router), ((0, 0), (0, other.shape[1] - part)))
    in_sent = jnp.concatenate([other, wide], axis=0)
    in_got = by_x(in_sent)
    in_near = added(mine, in_got[:capacity])
    in_blocks = over_z(
        plane_blocks(in_near, in_far, noted(router + read_note(in_got[capacity:])))
    )

    notes = jnp.concatenate([read_note(v) for v in in_blocks[:, capacity:]])
    grad_gate = jnp.sum(jnp.where(hot, notes[:, None], F32(0.0)), axis=0) / gate_prob
    mixed = (gate_prob[:, None] * placed(out_blocks)).astype(BF)
    grad_tokens = placed(in_blocks).astype(BF)

    d_gate_own, d_gate_rem, d_up_own, d_up_rem, _ = lax.optimization_barrier(
        (d_gate_own, d_gate_rem, d_up_own, d_up_rem, in_sent)
    )
    hidden_own, hidden_rem, _ = lax.optimization_barrier((hidden_own, hidden_rem, in_sent))
    x_keep, x_give = (jnp.concatenate([own, rem], axis=0) for own, rem in zip(x_own, x_rem))
    mine_all = jnp.concatenate([cot_own, cot_rem], axis=0)
    other_all = jnp.concatenate([cot_own_other, cot_rem_other], axis=0)
    d_gate_all = jnp.concatenate([d_gate_own, d_gate_rem], axis=0)
    d_up_all = jnp.concatenate([d_up_own, d_up_rem], axis=0)
    hidden_all = jnp.concatenate([hidden_own, hidden_rem], axis=0)

    def in_chip(keep, give):
        return keep + by_core(give.astype(BF)).astype(F32)

    grad_w_gate = in_chip(contract_rows(x_keep, d_gate_all), contract_rows(x_give, d_gate_all))
    grad_w_up = in_chip(contract_rows(x_keep, d_up_all), contract_rows(x_give, d_up_all))
    down_keep = jnp.concatenate([mine_all[:, :part], other_all[:, :part]], axis=1)
    down_give = jnp.concatenate([mine_all[:, part:], other_all[:, part:]], axis=1)
    grad_down = in_chip(contract_rows(hidden_all, down_keep), contract_rows(hidden_all, down_give))
    turned = jnp.concatenate([grad_down[:, part:], grad_down[:, :part]], axis=1)
    grad_w_down = jnp.where(x == 0, grad_down, turned)
    return (mixed, grad_tokens, grad_gate, grad_w_gate, grad_w_up, grad_w_down)


def solution(mesh):
    in_specs = (
        P("dp", None),
        P("dp", None),
        P("dp"),
        P("dp", "owner"),
        P("dp", "owner"),
        P("owner", "dp"),
        P("dp", "owner"),
    )
    out_specs = (
        P("dp", "owner"),
        P("dp", "owner"),
        P("dp"),
        P("dp", "owner"),
        P("dp", "owner"),
        P("owner", "dp"),
    )
    local = exchanged if (mesh.shape["dp"], mesh.shape["owner"]) == (4, 8) else gathered
    return jax.shard_map(local, mesh=mesh, in_specs=in_specs, out_specs=out_specs, check_vma=False)
```

```python
import jax
import jax.numpy as jnp
from jax import lax
from jax.experimental import pallas as pl
from jax.experimental.pallas import tpu as pltpu
from jax.sharding import PartitionSpec as P

EXPERTS = 4
XDEPTH = 1
COST = 1024
OWN_COST = 20 * 10**9
TERM_COST = 20 * 10**9
BF = jnp.bfloat16
F32 = jnp.float32


def contract_rows(left, right):
    return lax.dot_general(
        left, right, (((0,), (0,)), ((), ())), preferred_element_type=jnp.float32
    )


def contract_cols(left, right):
    return lax.dot_general(
        left, right, (((1,), (1,)), ((), ())), preferred_element_type=jnp.float32
    )


def dot(left, right):
    return jnp.dot(left, right, preferred_element_type=jnp.float32)


def gathered(tokens, route, gate_prob, w_gate, w_up, w_down, d_out):
    row_count = tokens.shape[0]
    capacity = 3 * row_count // 4
    pieces = lax.axis_size("owner") // EXPERTS
    expert = lax.axis_index("owner") // pieces
    full_gate, full_up, full_down = (
        lax.all_gather(w_gate, "dp", axis=0, tiled=True),
        lax.all_gather(w_up, "dp", axis=0, tiled=True),
        lax.all_gather(w_down, "dp", axis=1, tiled=True),
    )
    selected = route[:, 0] == expert
    slot_index = jnp.cumsum(selected.astype(jnp.int32)) - 1
    safe_index = jnp.maximum(slot_index, 0)
    slot_ids = jnp.arange(capacity, dtype=jnp.int32)
    one_hot = jnp.logical_and(slot_index[None, :] == slot_ids[:, None], selected[None, :])
    dispatch = one_hot.astype(jnp.bfloat16)
    slot_tokens = dot(dispatch, tokens).astype(jnp.bfloat16)
    slot_probs = jnp.sum(jnp.where(one_hot, gate_prob[None, :], jnp.float32(0.0)), axis=1)
    row_weights = jnp.where(selected, gate_prob, jnp.float32(0.0))
    gate_pre = dot(slot_tokens, full_gate)
    up_pre = dot(slot_tokens, full_up)
    sigma = jax.nn.sigmoid(gate_pre)
    active = gate_pre * sigma
    hidden = (active * up_pre).astype(jnp.bfloat16)
    expert_out = dot(hidden, full_down)
    row_terms = jnp.take(expert_out, safe_index, axis=0) * row_weights[:, None]
    mixed = lax.psum_scatter(
        row_terms.astype(jnp.bfloat16), "owner", scatter_dimension=1, tiled=True
    )
    d_full = lax.all_gather(d_out, "owner", axis=1, tiled=True)
    slot_cotangent = dot(dispatch, d_full)
    slot_router = jnp.sum(slot_cotangent * expert_out, axis=1)
    router_terms = jnp.where(selected, jnp.take(slot_router, safe_index), jnp.float32(0.0))
    grad_gate = lax.psum(router_terms, "owner")
    d_expert = (slot_probs[:, None] * slot_cotangent).astype(jnp.bfloat16)
    d_hidden = contract_cols(d_expert, full_down)
    d_gate_pre = (d_hidden * up_pre * sigma * (1.0 + gate_pre * (1.0 - sigma))).astype(jnp.bfloat16)
    d_up_pre = (d_hidden * active).astype(jnp.bfloat16)
    slot_input = contract_cols(d_gate_pre, full_gate) + contract_cols(d_up_pre, full_up)
    input_terms = jnp.where(
        selected[:, None], jnp.take(slot_input, safe_index, axis=0), jnp.float32(0.0)
    )
    grad_tokens = lax.psum_scatter(
        input_terms.astype(jnp.bfloat16), "owner", scatter_dimension=1, tiled=True
    )
    gate_term = contract_rows(slot_tokens, d_gate_pre)
    up_term = contract_rows(slot_tokens, d_up_pre)
    down_term = contract_rows(hidden, d_expert)
    grad_w_gate, grad_w_up, grad_w_down = (
        lax.psum_scatter(
            gate_term.astype(jnp.bfloat16), "dp", scatter_dimension=0, tiled=True
        ).astype(jnp.float32),
        lax.psum_scatter(
            up_term.astype(jnp.bfloat16), "dp", scatter_dimension=0, tiled=True
        ).astype(jnp.float32),
        lax.psum_scatter(
            down_term.astype(jnp.bfloat16), "dp", scatter_dimension=1, tiled=True
        ).astype(jnp.float32),
    )
    return (mixed, grad_tokens, grad_gate, grad_w_gate, grad_w_up, grad_w_down)


def swap(value, axis, bit):
    pairs = [(i, i ^ bit) for i in range(lax.axis_size(axis))]
    return lax.ppermute(value, axis, pairs)


def after(value, *others):
    return lax.optimization_barrier((value,) + others)[0]


class Line:
    def __init__(self, axis, depth):
        self.axis, self.depth, self.done = axis, depth, []

    def __call__(self, value, bit):
        if len(self.done) >= self.depth:
            value = after(value, self.done[-self.depth])
        self.done.append(swap(value, self.axis, bit))
        return self.done[-1]


def on_core(body, outs, *args, cost=COST):
    vmem = pl.BlockSpec(memory_space=pltpu.VMEM)
    return pl.pallas_call(
        body,
        out_shape=[jax.ShapeDtypeStruct(shape, kind) for shape, kind in outs],
        in_specs=[pl.BlockSpec(memory_space=pltpu.SMEM)] + [vmem] * (len(args) - 1),
        out_specs=[vmem] * len(outs),
        compiler_params=pltpu.CompilerParams(vmem_limit_bytes=32 * 1024 * 1024),
        cost_estimate=pl.CostEstimate(flops=cost, bytes_accessed=COST, transcendentals=0),
    )(*args)


BLOCK = 256


def project_kernel(x_ref, first, second, gate, core_gate, up, core_up, out, sent):
    x = x_ref[0]
    swap_rows = x == 1
    left = jnp.where(swap_rows, second[...], first[...])
    right = jnp.where(swap_rows, first[...], second[...])
    for i, (own, core) in enumerate(((gate, core_gate), (up, core_up))):
        size = own.shape[1]
        for j in range(0, size, BLOCK):
            value = dot(left, own[:, j:j + BLOCK]) + dot(right, core[:, j:j + BLOCK])
            out[:, i * size + j:i * size + j + BLOCK] = value
            sent[:, i * size + j:i * size + j + BLOCK] = value.astype(BF)


def output_kernel(x_ref, hidden, down, core_down, mine, other):
    x = x_ref[0]
    part = down.shape[1] // 2
    for k, weight in enumerate((down, core_down)):
        for j in range(0, part, BLOCK):
            def cols(half):
                return weight[:, pl.ds(pl.multiple_of(half * part + j, BLOCK), BLOCK)]

            at = slice(k * part + j, k * part + j + BLOCK)
            mine[:, at] = dot(hidden[...], cols(x))
            other[:, at] = dot(hidden[...], cols(1 - x)).astype(BF)


def back_kernel(x_ref, mine, other, down, core_down, out, sent):
    x = x_ref[0]
    part = down.shape[1] // 2
    for j in range(0, down.shape[0], BLOCK):
        value = jnp.zeros((mine.shape[0], BLOCK), F32)
        for k, weight in enumerate((down, core_down)):
            for half, cot in ((x, mine), (1 - x, other)):
                cols = weight[j:j + BLOCK, pl.ds(pl.multiple_of(half * part, BLOCK), part)]
                value = value + contract_cols(cot[:, k * part:(k + 1) * part], cols)
        out[:, j:j + BLOCK] = value
        sent[:, j:j + BLOCK] = value.astype(BF)


def input_kernel(x_ref, d_gate, d_up, gate, core_gate, up, core_up, mine, other):
    x = x_ref[0]
    part = gate.shape[0] // 2
    for k, (gate_k, up_k) in enumerate(((gate, up), (core_gate, core_up))):
        for j in range(0, part, BLOCK):
            def value(half):
                at = pl.ds(pl.multiple_of(half * part + j, BLOCK), BLOCK)
                return contract_cols(d_gate[...], gate_k[at, :]) + contract_cols(d_up[...], up_k[at, :])

            at = slice(k * part + j, k * part + j + BLOCK)
            mine[:, at] = value(x)
            other[:, at] = value(1 - x).astype(BF)


def terms_kernel(
    x_ref, hidden, hidden_rem, mine, mine_rem, other, other_rem,
    tokens, got, swapped, d_gate, d_gate_rem, d_up, d_up_rem, down, gate, up
):
    part = mine.shape[1] // 2
    for half, (own, rem) in enumerate(((mine, mine_rem), (other, other_rem))):
        for j in range(0, part, BLOCK):
            at = slice(part + j, part + j + BLOCK)
            value = contract_rows(hidden[...], own[:, at]) + contract_rows(hidden_rem[...], rem[:, at])
            down[:, half * part + j:half * part + j + BLOCK] = value.astype(BF)
    tokens_rem = jnp.where(x_ref[0] == 1, got[...], swapped[...])
    for out, own, rem in ((gate, d_gate, d_gate_rem), (up, d_up, d_up_rem)):
        for j in range(0, out.shape[1], BLOCK):
            at = slice(j, j + BLOCK)
            value = contract_rows(tokens[...], own[:, at]) + contract_rows(tokens_rem, rem[:, at])
            out[:, at] = value.astype(BF)


def route_kernel(at_ref, route, tokens, own_place, place, sent):
    rows, capacity = route.shape[1], own_place.shape[0]
    chosen = route[...]
    member = lax.broadcasted_iota(jnp.int32, (8, rows), 0) == chosen
    member = jnp.where(member, F32(1.0), F32(0.0))
    row, col = (lax.broadcasted_iota(jnp.int32, (rows, rows), i) for i in (0, 1))
    upto = jnp.where(row <= col, F32(1.0), F32(0.0)).astype(BF)
    rank = jnp.sum(member * dot(member.astype(BF), upto), axis=0, keepdims=True) - 1.0
    slot = rank.astype(jnp.int32) + chosen * capacity

    def one_hot(count, first):
        ids = lax.broadcasted_iota(jnp.int32, (count, rows), 0) + first
        return jnp.where(ids == slot, F32(1.0), F32(0.0)).astype(BF)

    place[...] = one_hot(place.shape[0], 0)
    own_place[...] = one_hot(capacity, at_ref[0] * capacity)
    sent[...] = dot(own_place[...], tokens[...]).astype(BF)


def routed(at, route, tokens, capacity, quarter):
    rows = route.shape[1]
    shapes = ((capacity, rows), (EXPERTS * capacity, rows), (capacity, quarter))
    return pl.pallas_call(
        route_kernel,
        out_shape=[jax.ShapeDtypeStruct(shape, BF) for shape in shapes],
        grid_spec=pltpu.PrefetchScalarGridSpec(
            num_scalar_prefetch=1,
            grid=(1,),
            in_specs=[
                pl.BlockSpec((1, rows), lambda i, at: (0, 0)),
                pl.BlockSpec((rows, quarter), lambda i, at: (0, at[1])),
            ],
            out_specs=[pl.BlockSpec(shape, lambda i, at: (0, 0)) for shape in shapes],
        ),
        compiler_params=pltpu.CompilerParams(vmem_limit_bytes=32 * 1024 * 1024),
        cost_estimate=pl.CostEstimate(flops=COST, bytes_accessed=COST, transcendentals=0),
    )(at, route, tokens)


def take_cols(value, index, width):
    return lax.dynamic_slice_in_dim(value, index * width, width, axis=1)


def exchanged(tokens, route, gate_prob, w_gate, w_up, w_down, d_out):
    rows, width = tokens.shape
    capacity = 3 * rows // 4
    quarter = width // 4
    part = d_out.shape[1]
    d = lax.axis_index("dp")
    owner = lax.axis_index("owner")
    z, x = owner // 2, owner % 2
    y_line, x_line = Line("dp", 1), Line("owner", XDEPTH)

    def by_core(value):
        return swap(value, "dp", 1)

    def by_y(value):
        return y_line(value, 2)

    def by_x(value):
        return x_line(value, 1)

    def over_z(blocks):
        groups = [[2 * i + j for i in range(EXPERTS)] for j in range(2)]
        return lax.all_to_all(blocks, "owner", 0, 0, tiled=True, axis_index_groups=groups)

    at = jnp.stack([z, d ^ (2 + x)])
    own_place, place, x_sent = routed(at, route.reshape(1, rows), tokens, capacity, quarter)

    def x_cols(k):
        return take_cols(tokens, d ^ k, quarter)

    x_got = by_y(x_sent)
    x_own = [dot(own_place, x_cols(k)).astype(BF) for k in (0, 1)]

    d_expert = (gate_prob[:, None] * d_out.astype(F32)).astype(BF)
    cot_sent = dot(place, after(d_expert, x_sent)).astype(BF)
    cot_got = over_z(cot_sent.reshape(EXPERTS, capacity, part))

    core_gate, core_up, core_down = by_core(w_gate), by_core(w_up), by_core(w_down)

    x_at, zero = jnp.reshape(x, (1,)), jnp.zeros((1,), jnp.int32)
    size = w_gate.shape[1]

    def projected(turned, first, second, cost):
        weights = (w_gate, core_gate, w_up, core_up)
        shape = (capacity, 2 * size)
        return on_core(project_kernel, ((shape, F32), (shape, BF)), turned, first, second, *weights, cost=cost)

    part_own, sent_own = projected(zero, *x_own, OWN_COST)
    far_rem = by_y(sent_own)
    x_got = after(x_got, sent_own)
    x_other = by_x(x_got)
    def cot_at(k):
        return lax.dynamic_index_in_dim(cot_got, d ^ k, axis=0, keepdims=False)

    cot_far = jnp.concatenate([cot_at(2), cot_at(3)], axis=1)
    cot_own = jnp.concatenate([cot_at(0), cot_at(1)], axis=1)
    cot_rem = by_y(cot_far)
    cot_own_other = by_x(cot_own)

    x_got, x_other, _, _ = lax.optimization_barrier((x_got, x_other, cot_far, cot_own))
    part_rem, sent_rem = projected(x_at, x_got, x_other, COST)
    far_own = by_y(sent_rem)

    def back_of(mine, other):
        shape = (capacity, size)
        return on_core(back_kernel, ((shape, F32), (shape, BF)), x_at, mine, other, w_down, core_down)

    def forward(pair, far):
        pre = pair + far.astype(F32)
        gate_pre, up_pre = pre[:, :size], pre[:, size:]
        sigma = jax.nn.sigmoid(gate_pre)
        active = gate_pre * sigma
        return gate_pre, up_pre, sigma, active, (active * up_pre).astype(BF)

    def backward(pre, back, far):
        gate_pre, up_pre, sigma, active, hidden = pre
        d_hidden = back + far.astype(F32)
        d_gate = (d_hidden * up_pre * sigma * (1.0 + gate_pre * (1.0 - sigma))).astype(BF)
        d_up = (d_hidden * active).astype(BF)
        return d_gate, d_up, jnp.sum(hidden.astype(F32) * d_hidden, axis=1)

    pre_own, pre_rem = forward(part_own, far_own), forward(part_rem, far_rem)
    hidden_own, hidden_rem = pre_own[-1], pre_rem[-1]

    def added(mine, got):
        return (mine + got.astype(F32)).astype(BF)

    def output(hidden):
        shape = (capacity, 2 * part)
        return on_core(output_kernel, ((shape, F32), (shape, BF)), x_at, hidden, w_down, core_down)

    def d_input(d_gate, d_up):
        weights = (w_gate, core_gate, w_up, core_up)
        shape = (capacity, 2 * part)
        return on_core(input_kernel, ((shape, F32), (shape, BF)), x_at, d_gate, d_up, *weights)

    def plane_blocks(near, far, note=None):
        blocks = jnp.stack([near[:, :part], near[:, part:], far[:, :part], far[:, part:]])
        sent = [lax.dynamic_index_in_dim(blocks, d ^ i, axis=0, keepdims=True) for i in range(EXPERTS)]
        sent = jnp.concatenate(sent, axis=0)
        if note is not None:
            sent = jnp.concatenate([sent, jnp.broadcast_to(note, (EXPERTS, *note.shape))], axis=1)
        return sent

    def placed(got):
        return contract_rows(place, got[:, :capacity].reshape(EXPERTS * capacity, part))

    def noted(value):
        first = value.astype(BF)
        second = (value - first.astype(F32)).astype(BF)
        third = (value - first.astype(F32) - second.astype(F32)).astype(BF)
        lines = jnp.stack([first, second, third])
        return jnp.pad(lines, ((0, 13), (0, part - value.shape[0])))

    def read_note(lines):
        return jnp.sum(lines[:3, :capacity].astype(F32), axis=0)

    mine, other = output(hidden_rem)
    out_rem = added(mine, by_x(other))
    back_own, back_sent = back_of(cot_own, cot_own_other)
    back_far_rem = by_y(after(back_sent, out_rem))
    out_far = by_y(out_rem)
    cot_rem_other = by_x(cot_rem)
    out_mine, out_other = output(hidden_own)
    out_near = added(out_mine, by_x(out_other))
    back_rem, back_sent = back_of(cot_rem, after(cot_rem_other, back_far_rem))
    out_sent = plane_blocks(out_near, out_far)
    out_blocks = over_z(out_sent)
    back_far_own = by_y(after(back_sent, out_near))
    back_far_own = after(back_far_own, out_sent)

    d_gate_rem, d_up_rem, _ = backward(pre_rem, back_rem, back_far_rem)
    d_gate_own, d_up_own, router = backward(pre_own, back_own, back_far_own)
    mine, other = d_input(d_gate_rem, d_up_rem)
    in_rem = added(mine, by_x(other))
    in_far = by_y(in_rem)
    back_far_own = after(back_far_own, in_rem)
    mine, other = d_input(d_gate_own, d_up_own)
    wide = jnp.pad(noted(router), ((0, 0), (0, other.shape[1] - part)))
    in_sent = jnp.concatenate([other, wide], axis=0)
    in_got = by_x(in_sent)
    in_near = added(mine, in_got[:capacity])
    in_planes = plane_blocks(in_near, in_far, noted(router + read_note(in_got[capacity:])))
    in_blocks = over_z(in_planes)

    notes = jnp.concatenate([read_note(v) for v in in_blocks[:, capacity:]])
    grad_gate = jnp.sum(place.astype(F32) * notes[:, None], axis=0) / gate_prob
    mixed = (gate_prob[:, None] * placed(out_blocks)).astype(BF)
    grad_tokens = placed(in_blocks).astype(BF)

    def held(mark, *values):
        return lax.optimization_barrier((*values, mark))[:-1]

    def tall(own, rem):
        return jnp.concatenate([own, rem], axis=0)

    def down_term(mark, k):
        hidden_1, hidden_2, mine_1, mine_2, other_1, other_2 = held(
            mark, hidden_own, hidden_rem, cot_own, cot_rem, cot_own_other, cot_rem_other
        )
        at = slice(k * part, (k + 1) * part)
        rows_mine, rows_other = tall(mine_1[:, at], mine_2[:, at]), tall(other_1[:, at], other_2[:, at])
        return contract_rows(tall(hidden_1, hidden_2), jnp.concatenate([rows_mine, rows_other], axis=1))

    def token_term(mark, k, own, rem):
        x_1, got, other, grad_1, grad_2 = held(mark, x_own[k], x_got, x_other, own, rem)
        x_2 = jnp.where(x == k, got, other)
        return contract_rows(tall(x_1, x_2), tall(grad_1, grad_2))

    def in_chip(keep, give):
        return keep + by_core(give.astype(BF)).astype(F32)

    grads_gate, grads_up = (d_gate_own, d_gate_rem), (d_up_own, d_up_rem)
    terms = held(
        in_sent, hidden_own, hidden_rem, cot_own, cot_rem, cot_own_other, cot_rem_other,
        x_own[1], x_got, x_other, *grads_gate, *grads_up
    )
    outs = (((size, 2 * part), BF), ((quarter, size), BF), ((quarter, size), BF))
    give_down, give_gate, give_up = on_core(terms_kernel, outs, x_at, *terms, cost=TERM_COST)
    grad_w_gate = in_chip(token_term(in_planes, 0, *grads_gate), give_gate)
    grad_w_up = in_chip(token_term(in_planes, 0, *grads_up), give_up)
    grad_down = in_chip(down_term(in_planes, 0), give_down)
    turned = jnp.concatenate([grad_down[:, part:], grad_down[:, :part]], axis=1)
    grad_w_down = jnp.where(x == 0, grad_down, turned)
    return (mixed, grad_tokens, grad_gate, grad_w_gate, grad_w_up, grad_w_down)


def solution(mesh):
    in_specs = (
        P("dp", None),
        P("dp", None),
        P("dp"),
        P("dp", "owner"),
        P("dp", "owner"),
        P("owner", "dp"),
        P("dp", "owner"),
    )
    out_specs = (
        P("dp", "owner"),
        P("dp", "owner"),
        P("dp"),
        P("dp", "owner"),
        P("dp", "owner"),
        P("owner", "dp"),
    )
    local = exchanged if (mesh.shape["dp"], mesh.shape["owner"]) == (4, 8) else gathered
    return jax.shard_map(local, mesh=mesh, in_specs=in_specs, out_specs=out_specs, check_vma=False)
```

```python
import jax
import jax.numpy as jnp
from jax import lax
from jax.experimental import pallas as pl
from jax.experimental.pallas import tpu as pltpu
from jax.sharding import PartitionSpec as P

EXPERTS = 4
XDEPTH = 1
COST = 1024
OWN_COST = 20 * 10**9
TERM_COST = 8 * 10**9
BF = jnp.bfloat16
F32 = jnp.float32


def contract_rows(left, right):
    return lax.dot_general(
        left, right, (((0,), (0,)), ((), ())), preferred_element_type=jnp.float32
    )


def contract_cols(left, right):
    return lax.dot_general(
        left, right, (((1,), (1,)), ((), ())), preferred_element_type=jnp.float32
    )


def dot(left, right):
    return jnp.dot(left, right, preferred_element_type=jnp.float32)


def gathered(tokens, route, gate_prob, w_gate, w_up, w_down, d_out):
    row_count = tokens.shape[0]
    capacity = 3 * row_count // 4
    pieces = lax.axis_size("owner") // EXPERTS
    expert = lax.axis_index("owner") // pieces
    full_gate, full_up, full_down = (
        lax.all_gather(w_gate, "dp", axis=0, tiled=True),
        lax.all_gather(w_up, "dp", axis=0, tiled=True),
        lax.all_gather(w_down, "dp", axis=1, tiled=True),
    )
    selected = route[:, 0] == expert
    slot_index = jnp.cumsum(selected.astype(jnp.int32)) - 1
    safe_index = jnp.maximum(slot_index, 0)
    slot_ids = jnp.arange(capacity, dtype=jnp.int32)
    one_hot = jnp.logical_and(slot_index[None, :] == slot_ids[:, None], selected[None, :])
    dispatch = one_hot.astype(jnp.bfloat16)
    slot_tokens = dot(dispatch, tokens).astype(jnp.bfloat16)
    slot_probs = jnp.sum(jnp.where(one_hot, gate_prob[None, :], jnp.float32(0.0)), axis=1)
    row_weights = jnp.where(selected, gate_prob, jnp.float32(0.0))
    gate_pre = dot(slot_tokens, full_gate)
    up_pre = dot(slot_tokens, full_up)
    sigma = jax.nn.sigmoid(gate_pre)
    active = gate_pre * sigma
    hidden = (active * up_pre).astype(jnp.bfloat16)
    expert_out = dot(hidden, full_down)
    row_terms = jnp.take(expert_out, safe_index, axis=0) * row_weights[:, None]
    mixed = lax.psum_scatter(
        row_terms.astype(jnp.bfloat16), "owner", scatter_dimension=1, tiled=True
    )
    d_full = lax.all_gather(d_out, "owner", axis=1, tiled=True)
    slot_cotangent = dot(dispatch, d_full)
    slot_router = jnp.sum(slot_cotangent * expert_out, axis=1)
    router_terms = jnp.where(selected, jnp.take(slot_router, safe_index), jnp.float32(0.0))
    grad_gate = lax.psum(router_terms, "owner")
    d_expert = (slot_probs[:, None] * slot_cotangent).astype(jnp.bfloat16)
    d_hidden = contract_cols(d_expert, full_down)
    d_gate_pre = (d_hidden * up_pre * sigma * (1.0 + gate_pre * (1.0 - sigma))).astype(jnp.bfloat16)
    d_up_pre = (d_hidden * active).astype(jnp.bfloat16)
    slot_input = contract_cols(d_gate_pre, full_gate) + contract_cols(d_up_pre, full_up)
    input_terms = jnp.where(
        selected[:, None], jnp.take(slot_input, safe_index, axis=0), jnp.float32(0.0)
    )
    grad_tokens = lax.psum_scatter(
        input_terms.astype(jnp.bfloat16), "owner", scatter_dimension=1, tiled=True
    )
    gate_term = contract_rows(slot_tokens, d_gate_pre)
    up_term = contract_rows(slot_tokens, d_up_pre)
    down_term = contract_rows(hidden, d_expert)
    grad_w_gate, grad_w_up, grad_w_down = (
        lax.psum_scatter(
            gate_term.astype(jnp.bfloat16), "dp", scatter_dimension=0, tiled=True
        ).astype(jnp.float32),
        lax.psum_scatter(
            up_term.astype(jnp.bfloat16), "dp", scatter_dimension=0, tiled=True
        ).astype(jnp.float32),
        lax.psum_scatter(
            down_term.astype(jnp.bfloat16), "dp", scatter_dimension=1, tiled=True
        ).astype(jnp.float32),
    )
    return (mixed, grad_tokens, grad_gate, grad_w_gate, grad_w_up, grad_w_down)


def swap(value, axis, bit):
    pairs = [(i, i ^ bit) for i in range(lax.axis_size(axis))]
    return lax.ppermute(value, axis, pairs)


def after(value, *others):
    return lax.optimization_barrier((value,) + others)[0]


class Line:
    def __init__(self, axis, depth):
        self.axis, self.depth, self.done = axis, depth, []

    def __call__(self, value, bit):
        if len(self.done) >= self.depth:
            value = after(value, self.done[-self.depth])
        self.done.append(swap(value, self.axis, bit))
        return self.done[-1]


def on_core(body, outs, *args, cost=COST):
    vmem = pl.BlockSpec(memory_space=pltpu.VMEM)
    return pl.pallas_call(
        body,
        out_shape=[jax.ShapeDtypeStruct(shape, kind) for shape, kind in outs],
        in_specs=[pl.BlockSpec(memory_space=pltpu.SMEM)] + [vmem] * (len(args) - 1),
        out_specs=[vmem] * len(outs),
        compiler_params=pltpu.CompilerParams(vmem_limit_bytes=32 * 1024 * 1024),
        cost_estimate=pl.CostEstimate(flops=cost, bytes_accessed=COST, transcendentals=0),
    )(*args)


BLOCK = 256


def project_kernel(x_ref, first, second, gate, core_gate, up, core_up, out, sent):
    x = x_ref[0]
    swap_rows = x == 1
    left = jnp.where(swap_rows, second[...], first[...])
    right = jnp.where(swap_rows, first[...], second[...])
    for i, (own, core) in enumerate(((gate, core_gate), (up, core_up))):
        size = own.shape[1]
        for j in range(0, size, BLOCK):
            value = dot(left, own[:, j:j + BLOCK]) + dot(right, core[:, j:j + BLOCK])
            out[:, i * size + j:i * size + j + BLOCK] = value
            sent[:, i * size + j:i * size + j + BLOCK] = value.astype(BF)


def output_kernel(x_ref, hidden, down, core_down, mine, other):
    x = x_ref[0]
    part = down.shape[1] // 2
    for k, weight in enumerate((down, core_down)):
        for j in range(0, part, BLOCK):
            def cols(half):
                return weight[:, pl.ds(pl.multiple_of(half * part + j, BLOCK), BLOCK)]

            at = slice(k * part + j, k * part + j + BLOCK)
            mine[:, at] = dot(hidden[...], cols(x)).astype(BF)
            other[:, at] = dot(hidden[...], cols(1 - x)).astype(BF)


def back_kernel(x_ref, mine, other, down, core_down, out, sent):
    x = x_ref[0]
    part = down.shape[1] // 2
    for j in range(0, down.shape[0], BLOCK):
        value = jnp.zeros((mine.shape[0], BLOCK), F32)
        for k, weight in enumerate((down, core_down)):
            for half, cot in ((x, mine), (1 - x, other)):
                cols = weight[j:j + BLOCK, pl.ds(pl.multiple_of(half * part, BLOCK), part)]
                value = value + contract_cols(cot[:, k * part:(k + 1) * part], cols)
        out[:, j:j + BLOCK] = value
        sent[:, j:j + BLOCK] = value.astype(BF)


def input_kernel(x_ref, d_gate, d_up, gate, core_gate, up, core_up, mine, other):
    x = x_ref[0]
    part = gate.shape[0] // 2
    for k, (gate_k, up_k) in enumerate(((gate, up), (core_gate, core_up))):
        for j in range(0, part, BLOCK):
            def value(half):
                at = pl.ds(pl.multiple_of(half * part + j, BLOCK), BLOCK)
                return contract_cols(d_gate[...], gate_k[at, :]) + contract_cols(d_up[...], up_k[at, :])

            at = slice(k * part + j, k * part + j + BLOCK)
            mine[:, at] = value(x).astype(BF)
            other[:, at] = value(1 - x).astype(BF)


def terms_kernel(
    x_ref, hidden, hidden_rem, mine, mine_rem, other, other_rem,
    tokens, got, swapped, d_gate, d_gate_rem, d_up, d_up_rem, down, gate, up
):
    part = mine.shape[1] // 2
    for half, (own, rem) in enumerate(((mine, mine_rem), (other, other_rem))):
        for j in range(0, part, BLOCK):
            at = slice(part + j, part + j + BLOCK)
            value = contract_rows(hidden[...], own[:, at]) + contract_rows(hidden_rem[...], rem[:, at])
            down[:, half * part + j:half * part + j + BLOCK] = value.astype(BF)
    tokens_rem = jnp.where(x_ref[0] == 1, got[...], swapped[...])
    for out, own, rem in ((gate, d_gate, d_gate_rem), (up, d_up, d_up_rem)):
        for j in range(0, out.shape[1], BLOCK):
            at = slice(j, j + BLOCK)
            value = contract_rows(tokens[...], own[:, at]) + contract_rows(tokens_rem, rem[:, at])
            out[:, at] = value.astype(BF)


def route_kernel(at_ref, route, tokens, own_place, place, sent):
    rows, capacity = route.shape[1], own_place.shape[0]
    chosen = route[...]
    member = lax.broadcasted_iota(jnp.int32, (8, rows), 0) == chosen
    member = jnp.where(member, F32(1.0), F32(0.0))
    row, col = (lax.broadcasted_iota(jnp.int32, (rows, rows), i) for i in (0, 1))
    upto = jnp.where(row <= col, F32(1.0), F32(0.0)).astype(BF)
    rank = jnp.sum(member * dot(member.astype(BF), upto), axis=0, keepdims=True) - 1.0
    slot = rank.astype(jnp.int32) + chosen * capacity

    def one_hot(count, first):
        ids = lax.broadcasted_iota(jnp.int32, (count, rows), 0) + first
        return jnp.where(ids == slot, F32(1.0), F32(0.0)).astype(BF)

    place[...] = one_hot(place.shape[0], 0)
    own_place[...] = one_hot(capacity, at_ref[0] * capacity)
    sent[...] = dot(own_place[...], tokens[...]).astype(BF)


def routed(at, route, tokens, capacity, quarter):
    rows = route.shape[1]
    shapes = ((capacity, rows), (EXPERTS * capacity, rows), (capacity, quarter))
    return pl.pallas_call(
        route_kernel,
        out_shape=[jax.ShapeDtypeStruct(shape, BF) for shape in shapes],
        grid_spec=pltpu.PrefetchScalarGridSpec(
            num_scalar_prefetch=1,
            grid=(1,),
            in_specs=[
                pl.BlockSpec((1, rows), lambda i, at: (0, 0)),
                pl.BlockSpec((rows, quarter), lambda i, at: (0, at[1])),
            ],
            out_specs=[pl.BlockSpec(shape, lambda i, at: (0, 0)) for shape in shapes],
        ),
        compiler_params=pltpu.CompilerParams(vmem_limit_bytes=32 * 1024 * 1024),
        cost_estimate=pl.CostEstimate(flops=COST, bytes_accessed=COST, transcendentals=0),
    )(at, route, tokens)


def take_cols(value, index, width):
    return lax.dynamic_slice_in_dim(value, index * width, width, axis=1)


def exchanged(tokens, route, gate_prob, w_gate, w_up, w_down, d_out):
    rows, width = tokens.shape
    capacity = 3 * rows // 4
    quarter = width // 4
    part = d_out.shape[1]
    d = lax.axis_index("dp")
    owner = lax.axis_index("owner")
    z, x = owner // 2, owner % 2
    y_line, x_line = Line("dp", 1), Line("owner", XDEPTH)

    def by_core(value):
        return swap(value, "dp", 1)

    def by_y(value):
        return y_line(value, 2)

    def by_x(value):
        return x_line(value, 1)

    def over_z(blocks):
        groups = [[2 * i + j for i in range(EXPERTS)] for j in range(2)]
        return lax.all_to_all(blocks, "owner", 0, 0, tiled=True, axis_index_groups=groups)

    at = jnp.stack([z, d ^ (2 + x)])
    own_place, place, x_sent = routed(at, route.reshape(1, rows), tokens, capacity, quarter)

    def x_cols(k):
        return take_cols(tokens, d ^ k, quarter)

    x_got = by_y(x_sent)
    x_own = [dot(own_place, x_cols(k)).astype(BF) for k in (0, 1)]

    d_expert = (gate_prob[:, None] * d_out.astype(F32)).astype(BF)
    cot_sent = dot(place, after(d_expert, x_sent)).astype(BF)
    cot_got = over_z(cot_sent.reshape(EXPERTS, capacity, part))

    core_gate, core_up, core_down = by_core(w_gate), by_core(w_up), by_core(w_down)

    x_at, zero = jnp.reshape(x, (1,)), jnp.zeros((1,), jnp.int32)
    size = w_gate.shape[1]

    def projected(turned, first, second, cost):
        weights = (w_gate, core_gate, w_up, core_up)
        shape = (capacity, 2 * size)
        return on_core(project_kernel, ((shape, F32), (shape, BF)), turned, first, second, *weights, cost=cost)

    part_own, sent_own = projected(zero, *x_own, OWN_COST)
    far_rem = by_y(sent_own)
    x_got = after(x_got, sent_own)
    x_other = by_x(x_got)
    def cot_at(k):
        return lax.dynamic_index_in_dim(cot_got, d ^ k, axis=0, keepdims=False)

    cot_far = jnp.concatenate([cot_at(2), cot_at(3)], axis=1)
    cot_own = jnp.concatenate([cot_at(0), cot_at(1)], axis=1)
    cot_rem = by_y(cot_far)
    cot_own_other = by_x(cot_own)

    x_got, x_other, _, _ = lax.optimization_barrier((x_got, x_other, cot_far, cot_own))
    part_rem, sent_rem = projected(x_at, x_got, x_other, COST)
    far_own = by_y(sent_rem)

    def back_of(mine, other):
        shape = (capacity, size)
        return on_core(back_kernel, ((shape, F32), (shape, BF)), x_at, mine, other, w_down, core_down)

    def forward(pair, far):
        pre = pair + far.astype(F32)
        gate_pre, up_pre = pre[:, :size], pre[:, size:]
        sigma = jax.nn.sigmoid(gate_pre)
        active = gate_pre * sigma
        return gate_pre, up_pre, sigma, active, (active * up_pre).astype(BF)

    def backward(pre, back, far):
        gate_pre, up_pre, sigma, active, hidden = pre
        d_hidden = back + far.astype(F32)
        d_gate = (d_hidden * up_pre * sigma * (1.0 + gate_pre * (1.0 - sigma))).astype(BF)
        d_up = (d_hidden * active).astype(BF)
        return d_gate, d_up, jnp.sum(hidden.astype(F32) * d_hidden, axis=1)

    pre_own, pre_rem = forward(part_own, far_own), forward(part_rem, far_rem)
    hidden_own, hidden_rem = pre_own[-1], pre_rem[-1]

    def added(mine, got):
        return (mine.astype(F32) + got.astype(F32)).astype(BF)

    def output(hidden):
        shape = (capacity, 2 * part)
        return on_core(output_kernel, ((shape, BF), (shape, BF)), x_at, hidden, w_down, core_down)

    def d_input(d_gate, d_up):
        weights = (w_gate, core_gate, w_up, core_up)
        shape = (capacity, 2 * part)
        return on_core(input_kernel, ((shape, BF), (shape, BF)), x_at, d_gate, d_up, *weights)

    def plane_blocks(near, far, note=None):
        blocks = jnp.stack([near[:, :part], near[:, part:], far[:, :part], far[:, part:]])
        sent = [lax.dynamic_index_in_dim(blocks, d ^ i, axis=0, keepdims=True) for i in range(EXPERTS)]
        sent = jnp.concatenate(sent, axis=0)
        if note is not None:
            sent = jnp.concatenate([sent, jnp.broadcast_to(note, (EXPERTS, *note.shape))], axis=1)
        return sent

    def placed(got):
        return contract_rows(place, got[:, :capacity].reshape(EXPERTS * capacity, part))

    def noted(value):
        first = value.astype(BF)
        second = (value - first.astype(F32)).astype(BF)
        third = (value - first.astype(F32) - second.astype(F32)).astype(BF)
        lines = jnp.stack([first, second, third])
        return jnp.pad(lines, ((0, 13), (0, part - value.shape[0])))

    def read_note(lines):
        return jnp.sum(lines[:3, :capacity].astype(F32), axis=0)

    mine, other = output(hidden_rem)
    out_rem = added(mine, by_x(other))
    back_own, back_sent = back_of(cot_own, cot_own_other)
    back_far_rem = by_y(after(back_sent, out_rem))
    out_far = by_y(out_rem)
    cot_rem_other = by_x(cot_rem)
    out_mine, out_other = output(hidden_own)
    out_near = added(out_mine, by_x(out_other))
    back_rem, back_sent = back_of(cot_rem, after(cot_rem_other, back_far_rem))
    out_sent = plane_blocks(out_near, out_far)
    out_blocks = over_z(out_sent)
    back_far_own = by_y(after(back_sent, out_near))
    back_far_own = after(back_far_own, out_sent)

    d_gate_rem, d_up_rem, _ = backward(pre_rem, back_rem, back_far_rem)
    d_gate_own, d_up_own, router = backward(pre_own, back_own, back_far_own)
    mine, other = d_input(d_gate_rem, d_up_rem)
    in_rem = added(mine, by_x(other))
    in_far = by_y(in_rem)
    back_far_own = after(back_far_own, in_rem)
    mine, other = d_input(d_gate_own, d_up_own)
    wide = jnp.pad(noted(router), ((0, 0), (0, other.shape[1] - part)))
    in_sent = jnp.concatenate([other, wide], axis=0)
    in_got = by_x(in_sent)
    in_near = added(mine, in_got[:capacity])
    in_planes = plane_blocks(in_near, in_far, noted(router + read_note(in_got[capacity:])))
    in_blocks = over_z(in_planes)

    notes = jnp.concatenate([read_note(v) for v in in_blocks[:, capacity:]])
    grad_gate = jnp.sum(place.astype(F32) * notes[:, None], axis=0) / gate_prob
    mixed = (gate_prob[:, None] * placed(out_blocks)).astype(BF)
    grad_tokens = placed(in_blocks).astype(BF)

    def held(mark, *values):
        return lax.optimization_barrier((*values, mark))[:-1]

    def tall(own, rem):
        return jnp.concatenate([own, rem], axis=0)

    def down_term(mark, k):
        hidden_1, hidden_2, mine_1, mine_2, other_1, other_2 = held(
            mark, hidden_own, hidden_rem, cot_own, cot_rem, cot_own_other, cot_rem_other
        )
        at = slice(k * part, (k + 1) * part)
        rows_mine, rows_other = tall(mine_1[:, at], mine_2[:, at]), tall(other_1[:, at], other_2[:, at])
        return contract_rows(tall(hidden_1, hidden_2), jnp.concatenate([rows_mine, rows_other], axis=1))

    def token_term(mark, k, own, rem):
        x_1, got, other, grad_1, grad_2 = held(mark, x_own[k], x_got, x_other, own, rem)
        x_2 = jnp.where(x == k, got, other)
        return contract_rows(tall(x_1, x_2), tall(grad_1, grad_2))

    def in_chip(keep, give):
        return keep + by_core(give.astype(BF)).astype(F32)

    grads_gate, grads_up = (d_gate_own, d_gate_rem), (d_up_own, d_up_rem)
    terms = held(
        in_sent, hidden_own, hidden_rem, cot_own, cot_rem, cot_own_other, cot_rem_other,
        x_own[1], x_got, x_other, *grads_gate, *grads_up
    )
    outs = (((size, 2 * part), BF), ((quarter, size), BF), ((quarter, size), BF))
    give_down, give_gate, give_up = on_core(terms_kernel, outs, x_at, *terms, cost=TERM_COST)
    grad_w_gate = in_chip(token_term(in_planes, 0, *grads_gate), give_gate)
    grad_w_up = in_chip(token_term(in_planes, 0, *grads_up), give_up)
    grad_down = in_chip(down_term(in_planes, 0), give_down)
    turned = jnp.concatenate([grad_down[:, part:], grad_down[:, :part]], axis=1)
    grad_w_down = jnp.where(x == 0, grad_down, turned)
    return (mixed, grad_tokens, grad_gate, grad_w_gate, grad_w_up, grad_w_down)


def solution(mesh):
    in_specs = (
        P("dp", None),
        P("dp", None),
        P("dp"),
        P("dp", "owner"),
        P("dp", "owner"),
        P("owner", "dp"),
        P("dp", "owner"),
    )
    out_specs = (
        P("dp", "owner"),
        P("dp", "owner"),
        P("dp"),
        P("dp", "owner"),
        P("dp", "owner"),
        P("owner", "dp"),
    )
    local = exchanged if (mesh.shape["dp"], mesh.shape["owner"]) == (4, 8) else gathered
    return jax.shard_map(local, mesh=mesh, in_specs=in_specs, out_specs=out_specs, check_vma=False)
```
